32 devices in a mesh: head: 4 (over x, core), ctx: 8 (over z, y).
Axes of the slice: x: 2, y: 2, z: 4, core: 2. Of those that a mesh axis runs over, the one named last changes fastest.
Arguments:
- query_rows: bfloat16 [4096, 4096], P(('head', 'ctx')), may hold values from -6 to 6
- key_rows: bfloat16 [4096, 4096], P(('head', 'ctx')), may hold values from -6 to 6
- value_rows: bfloat16 [4096, 4096], P(('head', 'ctx')), may hold values from -6 to 6
- token_rates: float32 [4096, 16], P(('head', 'ctx')), may hold values from 0.05 to 0.5
- fast_weights: float32 [16, 3, 1024, 256], P('head'), may hold values from -0.4 to 0.4
- momentum: float32 [16, 3, 1024, 256], P('head'), may hold values from -0.12 to 0.12
- out_weight: bfloat16 [4096, 4096], P('head'), may hold values from -0.09375 to 0.09375
Outputs:
- output: bfloat16 [4096, 4096], P(('head', 'ctx'))
The draws below stay inside these ranges and needn't reach their ends.
All inputs are finite; a program needn't handle non-finite values.
Results may differ from the reference program's by a relative error of at most 0.035.
Values may be sent and summed in bfloat16 or wider, within the bound.
No kernel may reach another device: no remote copies, remote signals or barrier semaphores. Data moves between devices by JAX's collectives and lax.ppermute only.
A program may use at most 128 MiB of HBM per device.

```python
import math
import jax
import jax.numpy as jnp
from jax import lax

HEADS = 16
D_H = 256
FF = 1024
D = 4096
TOKENS = 4096
N_HEAD = 4


def levels(rng, shape, shards, smallest, high):
    loudness, own = 1.0, jax.random.fold_in(rng, 6)
    for position, shards_of in shards:
        heights = jnp.exp(jax.random.uniform(jax.random.fold_in(own, position), (shards_of,), jnp.float32, smallest / len(shards), high / len(shards)))
        loudness = loudness * jnp.repeat(heights, shape[position] // shards_of).reshape([-1 if axis == position else 1 for axis in range(len(shape))])
    return loudness


def noise(stream_key, shape, width, bound, split=(), held_as=jnp.bfloat16):
    drawn = jax.random.normal(stream_key, shape, jnp.float32) * width
    if len(split) > 0:
        drawn = levels(stream_key, shape, split, -0.22, 0.18) * drawn
    return jnp.clip(drawn, min=-bound, max=bound).astype(held_as)


def setup_inputs(seed: int = 0) -> dict:
    streams_of = jax.random.split(jax.random.key(seed), 8)
    return {
        "query_rows": noise(streams_of[0], (TOKENS, D), 1.0, 6.0, ((0, 32),)),
        "key_rows": noise(streams_of[1], (TOKENS, D), 1.0, 6.0, ((0, 32),)),
        "value_rows": noise(streams_of[2], (TOKENS, D), 1.0, 6.0, ((0, 32),)),
        "token_rates": jnp.clip(jnp.exp(math.log(0.5) - 2.3025851 * jax.random.uniform(streams_of[3], (TOKENS, HEADS), jnp.float32) ** levels(streams_of[3], (TOKENS, HEADS), ((0, 32),), -0.2, 0.2)), 0.05, 0.5),
        "fast_weights": noise(streams_of[4], (HEADS, 3, FF, D_H), 0.0625, 0.4, ((0, 4),), jnp.float32),
        "momentum": noise(streams_of[5], (HEADS, 3, FF, D_H), 0.02, 0.12, ((0, 4),), jnp.float32),
        "out_weight": noise(streams_of[6], (D, D), D ** -0.5, 0.09375, ((0, 4),)),
    }


def head_gradient(key_head, value_head, rate_col, weight_bf, rate_scale):
    pre_act = jnp.dot(key_head, weight_bf[0].T, preferred_element_type=jnp.float32)
    gate_act = jnp.dot(key_head, weight_bf[1].T, preferred_element_type=jnp.float32)
    sigmoid_pre = jax.nn.sigmoid(pre_act)
    silu_pre = pre_act * sigmoid_pre
    hidden = (silu_pre * gate_act).astype(jnp.bfloat16)
    grad_out = (-(rate_col * rate_scale) * value_head.astype(jnp.float32)).astype(jnp.bfloat16)
    grad_hidden = jnp.dot(grad_out, weight_bf[2].T, preferred_element_type=jnp.float32)
    grad_pre = (grad_hidden * gate_act * (sigmoid_pre * (1.0 + pre_act * (1.0 - sigmoid_pre)))).astype(jnp.bfloat16)
    grad_gate = (grad_hidden * silu_pre).astype(jnp.bfloat16)
    return jnp.stack([jnp.dot(grad_pre.T, key_head, preferred_element_type=jnp.float32), jnp.dot(grad_gate.T, key_head, preferred_element_type=jnp.float32), jnp.dot(hidden.T, grad_out, preferred_element_type=jnp.float32)])

def rescale(updated, previous_rows, previous_full, column_new):
    row_old = jnp.sqrt(lax.optimization_barrier(jnp.sum(jnp.square(previous_rows[:, :2]), axis=3, keepdims=True)))
    row_new = lax.optimization_barrier(jnp.sum(jnp.square(updated[:, :2]), axis=3, keepdims=True))
    first = updated[:, :2] * row_old / jnp.sqrt(row_new + 1e-06)
    column_old = jnp.sqrt(lax.optimization_barrier(jnp.sum(jnp.square(previous_full[:, 2]), axis=1, keepdims=True)))
    second = updated[:, 2] * column_old / jnp.sqrt(column_new + 1e-06)
    return jnp.concatenate([first, second[:, None]], axis=1)

def apply_head(query_head, normed_head):
    pre_act = jnp.dot(query_head, normed_head[0].T, preferred_element_type=jnp.float32)
    gate_act = jnp.dot(query_head, normed_head[1].T, preferred_element_type=jnp.float32)
    hidden = (pre_act * jax.nn.sigmoid(pre_act) * gate_act).astype(jnp.bfloat16)
    return jnp.dot(hidden, normed_head[2], preferred_element_type=jnp.float32).astype(jnp.bfloat16)

def reference(query_rows, key_rows, value_rows, token_rates, fast_weights, momentum, out_weight):
    rate_scale = float(TOKENS) ** (-0.5)
    gradient_list = []
    for head_index in range(HEADS):
        lower = head_index * D_H
        weight_bf = fast_weights[head_index].astype(jnp.bfloat16)
        gradient_list.append(head_gradient(key_rows[:, lower:lower + D_H], value_rows[:, lower:lower + D_H], token_rates[:, head_index:head_index + 1], weight_bf, rate_scale))
    gradients = jnp.stack(gradient_list)
    updated = fast_weights - (0.9 * momentum + gradients)
    column_new = lax.optimization_barrier(jnp.sum(jnp.square(updated[:, 2]), axis=1, keepdims=True))
    normed = rescale(updated, fast_weights, fast_weights, column_new).astype(jnp.bfloat16)
    mixed_list = []
    for head_index in range(HEADS):
        lower = head_index * D_H
        mixed_list.append(apply_head(query_rows[:, lower:lower + D_H], normed[head_index]))
    mixed = jnp.concatenate(mixed_list, axis=1)
    group_width = D // N_HEAD
    accumulated = jnp.zeros((TOKENS, D), jnp.float32)
    for group_index in range(N_HEAD):
        lower = group_index * group_width
        partial_sum = jnp.dot(mixed[:, lower:lower + group_width], out_weight[lower:lower + group_width], preferred_element_type=jnp.float32).astype(jnp.bfloat16)
        partial_sum = lax.optimization_barrier(partial_sum)
        accumulated = accumulated + partial_sum.astype(jnp.float32)
    return accumulated.astype(jnp.bfloat16)
```

```python
import functools

import jax
import jax.numpy as jnp
from jax import lax
from jax.experimental import pallas as pl
from jax.experimental.pallas import tpu as pltpu
from jax.sharding import Mesh
from jax.sharding import PartitionSpec as P

NT = (((1,), (1,)), ((), ()))


def f32_dot(a, b):
    return jnp.dot(a, b, preferred_element_type=jnp.float32)


def gradient_kernel(blocks, tokens_ref, weight_ref, grad_ref):
    w1 = weight_ref[0].astype(jnp.bfloat16)
    w3 = weight_ref[1].astype(jnp.bfloat16)
    w2 = weight_ref[2].astype(jnp.bfloat16)
    sources, _, rows, width = tokens_ref.shape
    totals = [None] * 3
    for start in range(0, sources, blocks):
        keys = tokens_ref[start : start + blocks, 0].reshape(blocks * rows, width)
        grad_out = tokens_ref[start : start + blocks, 1].reshape(blocks * rows, width)
        pre = lax.dot_general(w1, keys, NT, preferred_element_type=jnp.float32)
        gate = lax.dot_general(w3, keys, NT, preferred_element_type=jnp.float32)
        grad_hidden = lax.dot_general(w2, grad_out, NT, preferred_element_type=jnp.float32)
        sig = jax.nn.sigmoid(pre)
        silu = pre * sig
        hidden = (silu * gate).astype(jnp.bfloat16)
        grad_pre = (grad_hidden * gate * (sig + silu * (1.0 - sig))).astype(jnp.bfloat16)
        grad_gate = (grad_hidden * silu).astype(jnp.bfloat16)
        parts = (f32_dot(grad_pre, keys), f32_dot(grad_gate, keys), f32_dot(hidden, grad_out))
        totals = [p if t is None else t + p for t, p in zip(totals, parts)]
    for m in range(3):
        grad_ref[m] = totals[m].astype(grad_ref.dtype)


def head_gradient(tokens, weight):
    sources, _, rows, width = tokens.shape
    units = weight.shape[1]
    block = min(256, units)
    macs = 6 * sources * rows * width * units
    return pl.pallas_call(
        functools.partial(gradient_kernel, max(1, min(sources, 512 // rows))),
        grid=(units // block,),
        in_specs=[
            pl.BlockSpec(tokens.shape, lambda f: (0, 0, 0, 0)),
            pl.BlockSpec((3, block, width), lambda f: (0, f, 0)),
        ],
        out_specs=pl.BlockSpec((3, block, width), lambda f: (0, f, 0)),
        out_shape=jax.ShapeDtypeStruct(weight.shape, jnp.bfloat16),
        compiler_params=pltpu.CompilerParams(vmem_limit_bytes=24 << 20),
        cost_estimate=pl.CostEstimate(
            flops=2 * macs, bytes_accessed=10 << 20, transcendentals=sources * rows * units
        ),
        name="head_gradient",
    )(tokens, weight)


def apply_kernel(query_ref, normed_ref, out_ref):
    blocks, _, rows, width = query_ref.shape
    query = query_ref[:, 0].reshape(blocks * rows, width)
    pre = lax.dot_general(query, normed_ref[0], NT, preferred_element_type=jnp.float32)
    gate = lax.dot_general(query, normed_ref[1], NT, preferred_element_type=jnp.float32)
    hidden = (pre * jax.nn.sigmoid(pre) * gate).astype(jnp.bfloat16)
    out_ref[...] = f32_dot(hidden, normed_ref[2]).astype(out_ref.dtype).reshape(out_ref.shape)


def apply_head(queries, part, normed):
    sources, _, rows, width = queries.shape
    units = normed.shape[1]
    blocks = max(1, min(sources, 256 // rows))
    macs = 3 * sources * rows * width * units
    return pl.pallas_call(
        apply_kernel,
        grid=(sources // blocks,),
        in_specs=[
            pl.BlockSpec((blocks, 1, rows, width), lambda b: (b, part, 0, 0)),
            pl.BlockSpec(normed.shape, lambda b: (0, 0, 0)),
        ],
        out_specs=pl.BlockSpec((blocks, rows, width), lambda b: (b, 0, 0)),
        out_shape=jax.ShapeDtypeStruct((sources, rows, width), jnp.bfloat16),
        compiler_params=pltpu.CompilerParams(vmem_limit_bytes=24 << 20),
        cost_estimate=pl.CostEstimate(
            flops=2 * macs, bytes_accessed=4 << 20, transcendentals=sources * rows * units
        ),
        name="apply_head",
    )(queries, normed)


def rescale(updated, previous):
    row_old = jnp.sqrt(jnp.sum(jnp.square(previous[:2]), axis=2, keepdims=True))
    row_new = jnp.sum(jnp.square(updated[:2]), axis=2, keepdims=True)
    first = updated[:2] * (row_old / jnp.sqrt(row_new + 1e-06))
    column_old = jnp.sqrt(jnp.sum(jnp.square(previous[2]), axis=0, keepdims=True))
    column_new = jnp.sum(jnp.square(updated[2]), axis=0, keepdims=True)
    second = updated[2] * (column_old / jnp.sqrt(column_new + 1e-06))
    return jnp.concatenate([first, second[None]], axis=0).astype(jnp.bfloat16)


def shards(query_rows, key_rows, value_rows, token_rates, fast_weights, momentum, out_weight):
    sides, heads_here = lax.axis_size("x"), lax.axis_size("hd")
    side, core, head = lax.axis_index("x"), lax.axis_index("core"), lax.axis_index("hd")
    copies = lax.axis_size("rep")
    per_device, _, units, width = fast_weights.shape
    rows = key_rows.shape[0]
    heads = key_rows.shape[1] // width
    rate_scale = float(rows * sides * 2 * heads_here * copies) ** (-0.5)
    swap = [(0, 1), (1, 0)]

    grad_out = (
        -(token_rates * rate_scale)[:, :, None]
        * value_rows.reshape(rows, heads, width).astype(jnp.float32)
    ).astype(jnp.bfloat16)
    payload = jnp.stack(
        [key_rows.reshape(rows, heads, width).transpose(1, 0, 2), grad_out.transpose(1, 0, 2)],
        axis=1,
    )
    tokens = lax.all_to_all(payload, ("x", "hd"), 0, 0, tiled=True)

    owner = head // per_device
    weight_own = lax.dynamic_index_in_dim(fast_weights, head % per_device, 0, keepdims=False)
    momentum_own = lax.dynamic_index_in_dim(momentum, head % per_device, 0, keepdims=False)
    weight = jnp.where(owner == core, weight_own, lax.ppermute(weight_own, "core", swap))
    moment = jnp.where(owner == core, momentum_own, lax.ppermute(momentum_own, "core", swap))
    out_weight_other = lax.ppermute(out_weight, "core", swap)

    strip = heads_here * width
    query_parts = []
    for step in range(sides):
        target = lax.rem(side - step + sides, sides)
        part = lax.dynamic_slice_in_dim(query_rows, target * strip, strip, 1)
        if step:
            part = lax.ppermute(part, "x", [(i, (i - step) % sides) for i in range(sides)])
        query_parts.append(part.reshape(rows, heads_here, width).transpose(1, 0, 2))
    query_ready = jnp.stack(query_parts, axis=1)
    tokens, query_ready = lax.optimization_barrier((tokens, query_ready))
    queries = lax.all_to_all(query_ready, "hd", 0, 0, tiled=True)

    gradient = head_gradient(tokens, weight)
    summed = gradient.astype(jnp.float32) + lax.ppermute(gradient, "core", swap).astype(
        jnp.float32
    )
    if copies > 1:
        summed = lax.psum(summed.astype(jnp.bfloat16), "rep").astype(jnp.float32)
    normed = rescale(weight - (0.9 * moment + summed), weight)

    def project(mixed):
        mine = lax.dynamic_slice_in_dim(mixed, core * per_device, per_device, 0)
        other = lax.dynamic_slice_in_dim(mixed, (1 - core) * per_device, per_device, 0)
        mine = mine.transpose(1, 0, 2).reshape(rows, per_device * width)
        other = other.transpose(1, 0, 2).reshape(rows, per_device * width)
        return f32_dot(mine, out_weight) + f32_dot(other, out_weight_other)

    received = []
    for step in [*range(1, sides), 0]:
        applied = apply_head(queries, step, normed)
        mixed = lax.all_to_all(applied, "hd", 0, 0, tiled=True)
        partial = project(mixed)
        if step:
            partial = lax.ppermute(
                partial.astype(jnp.bfloat16), "x", [(i, (i + step) % sides) for i in range(sides)]
            )
        received.append(partial.astype(jnp.float32))
    return functools.reduce(jnp.add, received).astype(jnp.bfloat16)


def solution(mesh):
    head_axis, ctx_axis = mesh.shape["head"], mesh.shape["ctx"]

    def run(query_rows, key_rows, value_rows, token_rates, fast_weights, momentum, out_weight):
        heads_here = fast_weights.shape[0] // (head_axis // 2)
        fine = Mesh(
            mesh.devices.reshape(head_axis // 2, 2, heads_here, ctx_axis // heads_here),
            ("x", "core", "hd", "rep"),
        )
        token_spec = P(("x", "core", "hd", "rep"), None)
        weight_spec = P(("x", "core"), None, None, None)
        return jax.shard_map(
            shards,
            mesh=fine,
            in_specs=(token_spec,) * 4 + (weight_spec, weight_spec, P(("x", "core"), None)),
            out_specs=token_spec,
            check_vma=False,
        )(query_rows, key_rows, value_rows, token_rates, fast_weights, momentum, out_weight)

    return run
```

```python
import functools

import jax
import jax.numpy as jnp
from jax import lax
from jax.experimental import pallas as pl
from jax.experimental.pallas import tpu as pltpu
from jax.sharding import Mesh
from jax.sharding import PartitionSpec as P

NT = (((1,), (1,)), ((), ()))
VMEM = 14 << 20
SMALL = pl.CostEstimate(flops=1024, bytes_accessed=1024, transcendentals=0)


def f32_dot(a, b):
    return jnp.dot(a, b, preferred_element_type=jnp.float32)


def sigmoid(x):
    return 0.5 * jnp.tanh(0.5 * x) + 0.5


def pack_kernel(scale, group, key_ref, value_ref, rate_ref, out_ref):
    rates = rate_ref[...].T
    width = out_ref.shape[3]
    columns = lax.broadcasted_iota(jnp.int32, rates.shape, 1)
    for i in range(group):
        head = pl.program_id(0) * group + i
        rate = jnp.sum(jnp.where(columns == head, rates, 0.0), axis=1, keepdims=True)
        piece = slice(i * width, (i + 1) * width)
        out_ref[i, 0] = key_ref[:, piece]
        out_ref[i, 1] = (-(rate * scale) * value_ref[:, piece].astype(jnp.float32)).astype(
            out_ref.dtype
        )


def pack(key_rows, value_rows, token_rates, width, scale):
    rows, columns = key_rows.shape
    heads = columns // width
    group = 4 if heads % 4 == 0 else 1
    return pl.pallas_call(
        functools.partial(pack_kernel, scale, group),
        grid=(heads // group,),
        in_specs=[
            pl.BlockSpec((rows, group * width), lambda h: (0, h)),
            pl.BlockSpec((rows, group * width), lambda h: (0, h)),
            pl.BlockSpec(token_rates.shape[::-1], lambda h: (0, 0)),
        ],
        out_specs=pl.BlockSpec((group, 2, rows, width), lambda h: (h, 0, 0, 0)),
        out_shape=jax.ShapeDtypeStruct((heads, 2, rows, width), key_rows.dtype),
        compiler_params=pltpu.CompilerParams(vmem_limit_bytes=VMEM),
        name="pack",
    )(*(pltpu.with_memory_space_constraint(a, pltpu.HBM) for a in (key_rows, value_rows)), token_rates.T)


def turn_kernel(side_ref, rows_ref, out_ref):
    width = out_ref.shape[3]
    for i in range(out_ref.shape[1]):
        out_ref[0, i] = rows_ref[:, i * width : (i + 1) * width]


def turn(query_rows, side, sides, width):
    rows, columns = query_rows.shape
    strip = columns // sides
    return pl.pallas_call(
        turn_kernel,
        grid_spec=pltpu.PrefetchScalarGridSpec(
            num_scalar_prefetch=1,
            grid=(sides,),
            in_specs=[
                pl.BlockSpec((rows, strip), lambda d, s: (0, lax.rem(s[0] - d + sides, sides)))
            ],
            out_specs=pl.BlockSpec((1, strip // width, rows, width), lambda d, s: (d, 0, 0, 0)),
        ),
        out_shape=jax.ShapeDtypeStruct((sides, strip // width, rows, width), query_rows.dtype),
        compiler_params=pltpu.CompilerParams(vmem_limit_bytes=VMEM),
        cost_estimate=SMALL,
        name="turn",
    )(side[None], pltpu.with_memory_space_constraint(query_rows, pltpu.HBM))


def hold_kernel(own_ref, other_ref, after_ref, out_ref, sems):
    core = lax.axis_index("core")
    depth = own_ref.shape[0]
    first = pltpu.make_async_copy(own_ref, out_ref.at[pl.ds(core * depth, depth)], sems.at[0])
    second = pltpu.make_async_copy(
        other_ref, out_ref.at[pl.ds((1 - core) * depth, depth)], sems.at[1]
    )
    first.start()
    second.start()
    first.wait()
    second.wait()


def hold(own, other, after):
    depth, columns = own.shape
    own = pltpu.with_memory_space_constraint(own, pltpu.HBM)
    other = pltpu.with_memory_space_constraint(other, pltpu.HBM)
    return pl.pallas_call(
        hold_kernel,
        in_specs=[pl.BlockSpec(memory_space=pltpu.HBM)] * 2 + [pl.BlockSpec(memory_space=pl.ANY)],
        out_specs=pl.BlockSpec(memory_space=pltpu.VMEM),
        out_shape=pltpu.VMEM((2 * depth, columns), own.dtype),
        scratch_shapes=[pltpu.SemaphoreType.DMA((2,))],
        compiler_params=pltpu.CompilerParams(vmem_limit_bytes=VMEM),
        cost_estimate=SMALL,
        name="hold",
    )(own, other, after)


def gradient_kernel(blocks, tokens_ref, weight_ref, grad_ref):
    w1, w3, w2 = (weight_ref[m].astype(jnp.bfloat16) for m in range(3))
    sources, _, rows, width = tokens_ref.shape
    totals = [None] * 3
    for start in range(0, sources, blocks):
        keys = tokens_ref[start : start + blocks, 0].reshape(blocks * rows, width)
        grad_out = tokens_ref[start : start + blocks, 1].reshape(blocks * rows, width)
        pre = lax.dot_general(w1, keys, NT, preferred_element_type=jnp.float32)
        gate = lax.dot_general(w3, keys, NT, preferred_element_type=jnp.float32)
        grad_hidden = lax.dot_general(w2, grad_out, NT, preferred_element_type=jnp.float32)
        sig = sigmoid(pre)
        silu = pre * sig
        hidden = (silu * gate).astype(jnp.bfloat16)
        grad_pre = (grad_hidden * gate * (sig + silu * (1.0 - sig))).astype(jnp.bfloat16)
        grad_gate = (grad_hidden * silu).astype(jnp.bfloat16)
        parts = (f32_dot(grad_pre, keys), f32_dot(grad_gate, keys), f32_dot(hidden, grad_out))
        totals = [p if t is None else t + p for t, p in zip(totals, parts)]
    for m in range(3):
        grad_ref[m] = totals[m].astype(grad_ref.dtype)


def head_gradient(tokens, weight):
    sources, _, rows, width = tokens.shape
    units = weight.shape[1]
    block = min(256, units)
    return pl.pallas_call(
        functools.partial(gradient_kernel, max(1, min(sources, 512 // rows))),
        grid=(units // block,),
        in_specs=[
            pl.BlockSpec(tokens.shape, lambda f: (0, 0, 0, 0)),
            pl.BlockSpec((3, block, width), lambda f: (0, f, 0)),
        ],
        out_specs=pl.BlockSpec((3, block, width), lambda f: (0, f, 0)),
        out_shape=jax.ShapeDtypeStruct(weight.shape, jnp.bfloat16),
        compiler_params=pltpu.CompilerParams(vmem_limit_bytes=VMEM),
        cost_estimate=SMALL,
        name="head_gradient",
    )(*(pltpu.with_memory_space_constraint(a, pltpu.HBM) for a in (tokens, weight)))


def update_kernel(terms, weight_ref, momentum_ref, *refs):
    out_ref = refs[-1]
    previous = weight_ref[0]
    change = 0.9 * momentum_ref[0]
    for ref in refs[:terms]:
        change = change + ref[0].astype(jnp.float32)
    updated = previous - change

    def scaled(axis):
        old = jnp.sum(jnp.square(previous), axis=axis, keepdims=True)
        new = jnp.sum(jnp.square(updated), axis=axis, keepdims=True)
        out_ref[0] = (updated * (jnp.sqrt(old) / jnp.sqrt(new + 1e-06))).astype(out_ref.dtype)

    @pl.when(pl.program_id(0) < 2)
    def _():
        scaled(1)

    @pl.when(pl.program_id(0) == 2)
    def _():
        scaled(0)


def update(weight, moment, gradients, after):
    _, units, width = weight.shape
    spec = pl.BlockSpec((1, units, width), lambda m: (m, 0, 0))
    return pl.pallas_call(
        functools.partial(update_kernel, len(gradients)),
        grid=(3,),
        in_specs=[spec] * (2 + len(gradients)) + [pl.BlockSpec(memory_space=pl.ANY)] * len(after),
        out_specs=spec,
        out_shape=jax.ShapeDtypeStruct(weight.shape, jnp.bfloat16),
        compiler_params=pltpu.CompilerParams(vmem_limit_bytes=VMEM),
        cost_estimate=SMALL,
        name="update",
    )(weight, moment, *gradients, *after)


def apply_kernel(part, offsets, normed_ref, query_ref, *refs):
    out_refs = refs[-len(offsets) :]
    head = lax.axis_index("hd")
    _, _, rows, _ = query_ref.shape
    group = max(1, min(len(offsets), 512 // rows))
    for start in range(0, len(offsets), group):
        picked = offsets[start : start + group]
        query = jnp.concatenate([query_ref[jnp.bitwise_xor(head, i), part] for i in picked], axis=0)
        pre = lax.dot_general(query, normed_ref[0], NT, preferred_element_type=jnp.float32)
        gate = lax.dot_general(query, normed_ref[1], NT, preferred_element_type=jnp.float32)
        hidden = (pre * sigmoid(pre) * gate).astype(jnp.bfloat16)
        out = f32_dot(hidden, normed_ref[2]).astype(jnp.bfloat16)
        for n in range(len(picked)):
            out_refs[start + n][...] = out[n * rows : (n + 1) * rows]


def apply_head(queries, part, offsets, normed, after):
    _, _, rows, width = queries.shape
    whole = pl.BlockSpec(memory_space=pltpu.VMEM)
    return pl.pallas_call(
        functools.partial(apply_kernel, part, offsets),
        in_specs=[whole, whole] + [pl.BlockSpec(memory_space=pl.ANY)] * len(after),
        out_specs=[whole] * len(offsets),
        out_shape=[jax.ShapeDtypeStruct((rows, width), jnp.bfloat16)] * len(offsets),
        compiler_params=pltpu.CompilerParams(vmem_limit_bytes=VMEM),
        cost_estimate=SMALL,
        name="apply_head",
    )(normed, queries, *after)


def project_kernel(block, start, terms, weight_ref, *refs):
    mixed_refs, out_ref, depth_ref = refs[:terms], refs[-2], refs[-1]
    head = lax.axis_index("hd")
    rows, width = mixed_refs[0].shape
    for i, ref in enumerate(mixed_refs):
        depth_ref[jnp.bitwise_xor(head, i)] = ref[...]
    mixed = jnp.concatenate([depth_ref[i] for i in range(len(mixed_refs))], axis=1)
    for first in range(0, out_ref.shape[1], block):
        part = f32_dot(mixed, weight_ref[:, start + first : start + first + block])
        out_ref[:, first : first + block] = part.astype(out_ref.dtype)


def project(mixed, weight, start, stop, dtype, after):
    rows, width = mixed[0].shape
    block = min(512, stop - start)
    whole = pl.BlockSpec(memory_space=pltpu.VMEM)
    weight = pltpu.with_memory_space_constraint(weight, pltpu.VMEM)
    return pl.pallas_call(
        functools.partial(project_kernel, block, start, len(mixed)),
        in_specs=[whole] * (1 + len(mixed)) + [pl.BlockSpec(memory_space=pl.ANY)] * len(after),
        out_specs=whole,
        out_shape=jax.ShapeDtypeStruct((rows, stop - start), dtype),
        scratch_shapes=[pltpu.VMEM((len(mixed), rows, width), mixed[0].dtype)],
        compiler_params=pltpu.CompilerParams(vmem_limit_bytes=VMEM),
        cost_estimate=SMALL,
        name="project",
    )(weight, *mixed, *after)


def shards(query_rows, key_rows, value_rows, token_rates, fast_weights, momentum, out_weight):
    sides, heads_here = lax.axis_size("x"), lax.axis_size("hd")
    side, core, head = lax.axis_index("x"), lax.axis_index("core"), lax.axis_index("hd")
    copies = lax.axis_size("rep")
    per_device, _, units, width = fast_weights.shape
    rows = key_rows.shape[0]
    rate_scale = float(rows * sides * 2 * heads_here * copies) ** (-0.5)
    swap = [(0, 1), (1, 0)]

    payload = pack(key_rows, value_rows, token_rates, width, rate_scale)
    tokens = lax.all_to_all(payload, ("x", "hd"), 0, 0, tiled=True)

    owned = head // per_device == core
    weight = lax.dynamic_index_in_dim(fast_weights, head % per_device, 0, keepdims=False)
    moment = lax.dynamic_index_in_dim(momentum, head % per_device, 0, keepdims=False)
    weight = jnp.where(owned, weight, lax.ppermute(weight, "core", swap))
    moment = jnp.where(owned, moment, lax.ppermute(moment, "core", swap))
    out_weight_other = lax.ppermute(out_weight, "core", swap)

    turned = turn(query_rows, side, sides, width)
    query_parts = [turned[0]] + [
        lax.ppermute(turned[d], "x", [(i, (i - d) % sides) for i in range(sides)])
        for d in range(1, sides)
    ]
    ready = jnp.stack(query_parts, axis=1)
    ready, weight, moment, _ = lax.optimization_barrier(
        (ready, weight, moment, tokens[0, 0, :16, :128])
    )
    queries = lax.all_to_all(ready, "hd", 0, 0, tiled=True)

    gradient = head_gradient(tokens, weight)
    gradients = [gradient, lax.ppermute(gradient, "core", swap)]
    if copies > 1:
        summed = gradients[0].astype(jnp.float32) + gradients[1].astype(jnp.float32)
        gradients = [lax.psum(summed.astype(jnp.bfloat16), "rep")]
    normed = update(weight, moment, gradients, [])
    half = heads_here // 2
    near, far = tuple([*range(1, half), 0]), tuple(range(half, heads_here))
    partner = [[(c, c ^ i) for c in range(heads_here)] for i in range(heads_here)]

    columns = out_weight.shape[1]
    spans = [(0, columns // 4), (columns // 4, columns)]
    received = [[] for _ in spans]
    after, held = [], None
    for step in [*range(1, sides), 0]:
        mixed = [None] * heads_here
        for offsets in (far, near):
            applied = apply_head(queries, step, offsets, normed, after)
            after = [applied[0]]
            if held is None:
                held = hold(out_weight, out_weight_other, applied[0])
            for i, block in zip(offsets, applied):
                mixed[i] = lax.ppermute(block, "hd", partner[i]) if i else block
        if step:
            for n, span in enumerate(spans):
                partial = project(mixed, held, *span, jnp.bfloat16, after)
                after = [partial]
                partial = lax.ppermute(
                    partial, "x", [(i, (i + step) % sides) for i in range(sides)]
                )
                received[n].append(partial)
        else:
            own = project(mixed, held, 0, columns, jnp.float32, after)
    sums = [functools.reduce(jnp.add, [p.astype(jnp.float32) for p in r]) for r in received]
    return (own + jnp.concatenate(sums, axis=1)).astype(jnp.bfloat16)


def solution(mesh):
    head_axis, ctx_axis = mesh.shape["head"], mesh.shape["ctx"]

    def run(query_rows, key_rows, value_rows, token_rates, fast_weights, momentum, out_weight):
        heads_here = fast_weights.shape[0] // (head_axis // 2)
        fine = Mesh(
            mesh.devices.reshape(head_axis // 2, 2, heads_here, ctx_axis // heads_here),
            ("x", "core", "hd", "rep"),
        )
        token_spec = P(("x", "core", "hd", "rep"), None)
        weight_spec = P(("x", "core"), None, None, None)
        return jax.shard_map(
            shards,
            mesh=fine,
            in_specs=(token_spec,) * 4 + (weight_spec, weight_spec, P(("x", "core"), None)),
            out_specs=token_spec,
            check_vma=False,
        )(query_rows, key_rows, value_rows, token_rates, fast_weights, momentum, out_weight)

    return run
```

```python
import functools

import jax
import jax.numpy as jnp
from jax import lax
from jax.experimental import pallas as pl
from jax.experimental.pallas import tpu as pltpu
from jax.sharding import Mesh
from jax.sharding import PartitionSpec as P

NT = (((1,), (1,)), ((), ()))
VMEM = 24 << 20
SMALL = pl.CostEstimate(flops=1024, bytes_accessed=1024, transcendentals=0)


def f32_dot(a, b):
    return jnp.dot(a, b, preferred_element_type=jnp.float32)


def sigmoid(x):
    return 0.5 * jnp.tanh(0.5 * x) + 0.5


def pack_kernel(scale, group, key_ref, value_ref, rate_ref, out_ref):
    rates = rate_ref[...].T
    width = out_ref.shape[3]
    columns = lax.broadcasted_iota(jnp.int32, rates.shape, 1)
    for i in range(group):
        head = pl.program_id(0) * group + i
        rate = jnp.sum(jnp.where(columns == head, rates, 0.0), axis=1, keepdims=True)
        piece = slice(i * width, (i + 1) * width)
        out_ref[i, 0] = key_ref[:, piece]
        out_ref[i, 1] = (-(rate * scale) * value_ref[:, piece].astype(jnp.float32)).astype(
            out_ref.dtype
        )


def pack(key_rows, value_rows, token_rates, width, scale):
    rows, columns = key_rows.shape
    heads = columns // width
    group = 4 if heads % 4 == 0 else 1
    return pl.pallas_call(
        functools.partial(pack_kernel, scale, group),
        grid=(heads // group,),
        in_specs=[
            pl.BlockSpec((rows, group * width), lambda h: (0, h)),
            pl.BlockSpec((rows, group * width), lambda h: (0, h)),
            pl.BlockSpec(token_rates.shape[::-1], lambda h: (0, 0)),
        ],
        out_specs=pl.BlockSpec((group, 2, rows, width), lambda h: (h, 0, 0, 0)),
        out_shape=jax.ShapeDtypeStruct((heads, 2, rows, width), key_rows.dtype),
        compiler_params=pltpu.CompilerParams(vmem_limit_bytes=VMEM),
        name="pack",
    )(
        *(
            pltpu.with_memory_space_constraint(a, pltpu.HBM)
            for a in (key_rows, value_rows, token_rates.T)
        )
    )


def turn_kernel(side_ref, rows_ref, out_ref):
    width = out_ref.shape[3]
    for i in range(out_ref.shape[1]):
        out_ref[0, i] = rows_ref[:, i * width : (i + 1) * width]


def turn(query_rows, side, sides, width):
    rows, columns = query_rows.shape
    strip = columns // sides
    return pl.pallas_call(
        turn_kernel,
        grid_spec=pltpu.PrefetchScalarGridSpec(
            num_scalar_prefetch=1,
            grid=(sides,),
            in_specs=[
                pl.BlockSpec((rows, strip), lambda d, s: (0, lax.rem(s[0] - d + sides, sides)))
            ],
            out_specs=pl.BlockSpec((1, strip // width, rows, width), lambda d, s: (d, 0, 0, 0)),
        ),
        out_shape=jax.ShapeDtypeStruct((sides, strip // width, rows, width), query_rows.dtype),
        compiler_params=pltpu.CompilerParams(vmem_limit_bytes=VMEM),
        cost_estimate=SMALL,
        name="turn",
    )(side[None], pltpu.with_memory_space_constraint(query_rows, pltpu.HBM))


def hold_kernel(start, own_ref, other_ref, after_ref, out_ref, sems):
    core = lax.axis_index("core")
    depth, count = own_ref.shape[0], out_ref.shape[1]
    copies = [
        pltpu.make_async_copy(
            ref.at[:, pl.ds(start, count)], out_ref.at[pl.ds(place * depth, depth)], sems.at[n]
        )
        for n, (ref, place) in enumerate(((own_ref, core), (other_ref, 1 - core)))
    ]
    for copy in copies:
        copy.start()
    for copy in copies:
        copy.wait()


def hold(own, other, start, stop, after):
    depth = own.shape[0]
    own = pltpu.with_memory_space_constraint(own, pltpu.HBM)
    other = pltpu.with_memory_space_constraint(other, pltpu.HBM)
    return pl.pallas_call(
        functools.partial(hold_kernel, start),
        in_specs=[pl.BlockSpec(memory_space=pltpu.HBM)] * 2 + [pl.BlockSpec(memory_space=pl.ANY)],
        out_specs=pl.BlockSpec(memory_space=pltpu.VMEM),
        out_shape=pltpu.VMEM((2 * depth, stop - start), own.dtype),
        scratch_shapes=[pltpu.SemaphoreType.DMA((2,))],
        compiler_params=pltpu.CompilerParams(vmem_limit_bytes=VMEM),
        cost_estimate=SMALL,
        name="hold",
    )(own, other, after)


def gradient_kernel(blocks, tokens_ref, weight_ref, grad_ref):
    w1, w3, w2 = (weight_ref[m].astype(jnp.bfloat16) for m in range(3))
    sources, _, rows, width = tokens_ref.shape
    totals = [None] * 3
    for start in range(0, sources, blocks):
        keys = tokens_ref[start : start + blocks, 0].reshape(blocks * rows, width)
        grad_out = tokens_ref[start : start + blocks, 1].reshape(blocks * rows, width)
        pre = lax.dot_general(w1, keys, NT, preferred_element_type=jnp.float32)
        gate = lax.dot_general(w3, keys, NT, preferred_element_type=jnp.float32)
        grad_hidden = lax.dot_general(w2, grad_out, NT, preferred_element_type=jnp.float32)
        sig = sigmoid(pre)
        silu = pre * sig
        hidden = (silu * gate).astype(jnp.bfloat16)
        grad_pre = (grad_hidden * gate * (sig + silu * (1.0 - sig))).astype(jnp.bfloat16)
        grad_gate = (grad_hidden * silu).astype(jnp.bfloat16)
        parts = (f32_dot(grad_pre, keys), f32_dot(grad_gate, keys), f32_dot(hidden, grad_out))
        totals = [p if t is None else t + p for t, p in zip(totals, parts)]
    for m in range(3):
        grad_ref[m] = totals[m].astype(grad_ref.dtype)


def head_gradient(tokens, weight):
    sources, _, rows, width = tokens.shape
    units = weight.shape[1]
    block = min(256, units)
    return pl.pallas_call(
        functools.partial(gradient_kernel, max(1, min(sources, 512 // rows))),
        grid=(units // block,),
        in_specs=[
            pl.BlockSpec(tokens.shape, lambda f: (0, 0, 0, 0)),
            pl.BlockSpec((3, block, width), lambda f: (0, f, 0)),
        ],
        out_specs=pl.BlockSpec((3, block, width), lambda f: (0, f, 0)),
        out_shape=jax.ShapeDtypeStruct(weight.shape, jnp.bfloat16),
        compiler_params=pltpu.CompilerParams(vmem_limit_bytes=VMEM),
        cost_estimate=SMALL,
        name="head_gradient",
    )(tokens, pltpu.with_memory_space_constraint(weight, pltpu.HBM))


def update_kernel(terms, weight_ref, momentum_ref, *refs):
    out_ref = refs[-1]
    previous = weight_ref[0]
    change = 0.9 * momentum_ref[0]
    for ref in refs[:terms]:
        change = change + ref[0].astype(jnp.float32)
    updated = previous - change

    def scaled(axis):
        old = jnp.sum(jnp.square(previous), axis=axis, keepdims=True)
        new = jnp.sum(jnp.square(updated), axis=axis, keepdims=True)
        out_ref[0] = (updated * (jnp.sqrt(old) / jnp.sqrt(new + 1e-06))).astype(out_ref.dtype)

    @pl.when(pl.program_id(0) < 2)
    def _():
        scaled(1)

    @pl.when(pl.program_id(0) == 2)
    def _():
        scaled(0)


def update(weight, moment, gradients, after):
    _, units, width = weight.shape
    spec = pl.BlockSpec((1, units, width), lambda m: (m, 0, 0))
    return pl.pallas_call(
        functools.partial(update_kernel, len(gradients)),
        grid=(3,),
        in_specs=[spec] * (2 + len(gradients)) + [pl.BlockSpec(memory_space=pl.ANY)] * len(after),
        out_specs=spec,
        out_shape=jax.ShapeDtypeStruct(weight.shape, jnp.bfloat16),
        compiler_params=pltpu.CompilerParams(vmem_limit_bytes=VMEM),
        cost_estimate=SMALL,
        name="update",
    )(weight, moment, *gradients, *after)


def apply_kernel(parts, offsets, normed_ref, query_ref, *refs):
    out_refs = refs[-len(offsets) :]
    head = lax.axis_index("hd")
    _, _, rows, _ = query_ref.shape
    group = max(1, min(len(offsets), 512 // rows))
    for p, part in enumerate(parts):
        for start in range(0, len(offsets), group):
            picked = offsets[start : start + group]
            query = jnp.concatenate(
                [query_ref[jnp.bitwise_xor(head, i), part] for i in picked], axis=0
            )
            pre = lax.dot_general(query, normed_ref[0], NT, preferred_element_type=jnp.float32)
            gate = lax.dot_general(query, normed_ref[1], NT, preferred_element_type=jnp.float32)
            hidden = (pre * sigmoid(pre) * gate).astype(jnp.bfloat16)
            out = f32_dot(hidden, normed_ref[2]).astype(jnp.bfloat16)
            for n in range(len(picked)):
                out_refs[start + n][p] = out[n * rows : (n + 1) * rows]


def apply_head(queries, parts, offsets, normed, after):
    _, _, rows, width = queries.shape
    whole = pl.BlockSpec(memory_space=pltpu.VMEM)
    shape = jax.ShapeDtypeStruct((len(parts), rows, width), jnp.bfloat16)
    return pl.pallas_call(
        functools.partial(apply_kernel, parts, offsets),
        in_specs=[whole, whole] + [pl.BlockSpec(memory_space=pl.ANY)] * len(after),
        out_specs=[whole] * len(offsets),
        out_shape=[shape] * len(offsets),
        compiler_params=pltpu.CompilerParams(vmem_limit_bytes=VMEM),
        cost_estimate=SMALL,
        name="apply_head",
    )(normed, queries, *after)


def project_kernel(places, pieces, *refs):
    terms = len(places)
    mixed_refs, out_ref, depth_ref = refs[:terms], refs[-2], refs[-1]
    head = lax.axis_index("hd")
    for i, (ref, place) in enumerate(zip(mixed_refs, places)):
        depth_ref[jnp.bitwise_xor(head, i)] = ref[place]
    mixed = jnp.concatenate([depth_ref[i] for i in range(terms)], axis=1)
    first = 0
    for weight_ref in refs[terms : terms + pieces]:
        columns = weight_ref.shape[1]
        block = 512 if columns % 512 == 0 else columns
        for start in range(0, columns, block):
            part = f32_dot(mixed, weight_ref[:, start : start + block])
            out_ref[:, first + start : first + start + block] = part.astype(out_ref.dtype)
        first += columns


def project(blocks, weights, dtype, after):
    mixed, places = zip(*blocks)
    _, rows, width = mixed[0].shape
    whole = pl.BlockSpec(memory_space=pltpu.VMEM)
    weights = [pltpu.with_memory_space_constraint(w, pltpu.VMEM) for w in weights]
    return pl.pallas_call(
        functools.partial(project_kernel, places, len(weights)),
        in_specs=[whole] * (len(mixed) + len(weights))
        + [pl.BlockSpec(memory_space=pl.ANY)] * len(after),
        out_specs=whole,
        out_shape=jax.ShapeDtypeStruct((rows, sum(w.shape[1] for w in weights)), dtype),
        scratch_shapes=[pltpu.VMEM((len(mixed), rows, width), mixed[0].dtype)],
        compiler_params=pltpu.CompilerParams(vmem_limit_bytes=VMEM),
        cost_estimate=SMALL,
        name="project",
    )(*mixed, *weights, *after)


def shards(query_rows, key_rows, value_rows, token_rates, fast_weights, momentum, out_weight):
    sides, heads_here = lax.axis_size("x"), lax.axis_size("hd")
    side, core, head = lax.axis_index("x"), lax.axis_index("core"), lax.axis_index("hd")
    copies = lax.axis_size("rep")
    per_device, _, units, width = fast_weights.shape
    rows = key_rows.shape[0]
    rate_scale = float(rows * sides * 2 * heads_here * copies) ** (-0.5)
    swap = [(0, 1), (1, 0)]

    payload = pack(key_rows, value_rows, token_rates, width, rate_scale)
    tokens = lax.all_to_all(payload, ("x", "hd"), 0, 0, tiled=True)

    owned = head // per_device == core
    weight = lax.dynamic_index_in_dim(fast_weights, head % per_device, 0, keepdims=False)
    moment = lax.dynamic_index_in_dim(momentum, head % per_device, 0, keepdims=False)
    weight = jnp.where(owned, weight, lax.ppermute(weight, "core", swap))
    moment = jnp.where(owned, moment, lax.ppermute(moment, "core", swap))
    out_weight_other = lax.ppermute(out_weight, "core", swap)

    turned = turn(query_rows, side, sides, width)
    query_parts = [turned[0]] + [
        lax.ppermute(turned[d], "x", [(i, (i - d) % sides) for i in range(sides)])
        for d in range(1, sides)
    ]
    ready = jnp.stack(query_parts, axis=1)
    ready, weight, moment, tokens = lax.optimization_barrier((ready, weight, moment, tokens))
    queries = lax.all_to_all(ready, "hd", 0, 0, tiled=True)

    gradient = head_gradient(tokens, weight)
    gradients = [gradient, lax.ppermute(gradient, "core", swap)]
    if copies > 1:
        summed = gradients[0].astype(jnp.float32) + gradients[1].astype(jnp.float32)
        gradients = [lax.psum(summed.astype(jnp.bfloat16), "rep")]
    normed = update(weight, moment, gradients, [])
    half = heads_here // 2
    near, far = tuple([*range(1, half), 0]), tuple(range(half, heads_here))
    partner = [[(c, c ^ i) for c in range(heads_here)] for i in range(heads_here)]

    columns = out_weight.shape[1]
    split = columns * 3 // 4
    steps = (*range(1, sides), 0)

    def spread(parts, offsets, after):
        applied = apply_head(queries, parts, offsets, normed, after)
        moved = [
            lax.ppermute(block, "hd", partner[i]) if i else block
            for i, block in zip(offsets, applied)
        ]
        return moved, applied[0]

    crossing, done = {}, None
    crossing[steps[0]], done = spread(steps[:1], far, [])
    local, done = spread(steps, near, [done])
    held = [hold(out_weight, out_weight_other, 0, split, done)]
    crossing[steps[1]], done = spread(steps[1:2], far, held)
    received = [[], []]
    for place, step in enumerate(steps):
        if step not in crossing:
            crossing[step], done = spread((step,), far, [done])
        blocks = [None] * heads_here
        for i, block in zip(near, local):
            blocks[i] = (block, place)
        for i, block in zip(far, crossing[step]):
            blocks[i] = (block, 0)
        if step:
            over = [(i, (i + step) % sides) for i in range(sides)]
            done = project(blocks, held[:1], jnp.bfloat16, [done])
            received[0].append(lax.ppermute(done, "x", over))
            if len(held) == 1:
                held.append(hold(out_weight, out_weight_other, split, columns, done))
            done = project(blocks, held[1:], jnp.bfloat16, [])
            received[1].append(lax.ppermute(done, "x", over))
        else:
            own = project(blocks, held, jnp.float32, [])
    sums = [functools.reduce(jnp.add, [p.astype(jnp.float32) for p in r]) for r in received]
    return (own + jnp.concatenate(sums, axis=1)).astype(jnp.bfloat16)


def solution(mesh):
    head_axis, ctx_axis = mesh.shape["head"], mesh.shape["ctx"]

    def run(query_rows, key_rows, value_rows, token_rates, fast_weights, momentum, out_weight):
        heads_here = fast_weights.shape[0] // (head_axis // 2)
        fine = Mesh(
            mesh.devices.reshape(head_axis // 2, 2, heads_here, ctx_axis // heads_here),
            ("x", "core", "hd", "rep"),
        )
        token_spec = P(("x", "core", "hd", "rep"), None)
        weight_spec = P(("x", "core"), None, None, None)
        return jax.shard_map(
            shards,
            mesh=fine,
            in_specs=(token_spec,) * 4 + (weight_spec, weight_spec, P(("x", "core"), None)),
            out_specs=token_spec,
            check_vma=False,
        )(query_rows, key_rows, value_rows, token_rates, fast_weights, momentum, out_weight)

    return run
```

```python
import functools

import jax
import jax.numpy as jnp
from jax import lax
from jax.experimental import pallas as pl
from jax.experimental.pallas import tpu as pltpu
from jax.sharding import Mesh
from jax.sharding import PartitionSpec as P

NT = (((1,), (1,)), ((), ()))
VMEM = 24 << 20
SMALL = pl.CostEstimate(flops=1024, bytes_accessed=1024, transcendentals=0)


def f32_dot(a, b):
    return jnp.dot(a, b, preferred_element_type=jnp.float32)


def sigmoid(x):
    return 0.5 * jnp.tanh(0.5 * x) + 0.5


def pack_kernel(scale, group, key_ref, value_ref, rate_ref, out_ref):
    rates = rate_ref[...].T
    width = out_ref.shape[3]
    columns = lax.broadcasted_iota(jnp.int32, rates.shape, 1)
    for i in range(group):
        head = pl.program_id(0) * group + i
        rate = jnp.sum(jnp.where(columns == head, rates, 0.0), axis=1, keepdims=True)
        piece = slice(i * width, (i + 1) * width)
        out_ref[i, 0] = key_ref[:, piece]
        out_ref[i, 1] = (-(rate * scale) * value_ref[:, piece].astype(jnp.float32)).astype(
            out_ref.dtype
        )


def pack(key_rows, value_rows, token_rates, width, scale):
    rows, columns = key_rows.shape
    heads = columns // width
    group = 8 if heads % 8 == 0 else 1
    return pl.pallas_call(
        functools.partial(pack_kernel, scale, group),
        grid=(heads // group,),
        in_specs=[
            pl.BlockSpec((rows, group * width), lambda h: (0, h)),
            pl.BlockSpec((rows, group * width), lambda h: (0, h)),
            pl.BlockSpec(token_rates.shape[::-1], lambda h: (0, 0)),
        ],
        out_specs=pl.BlockSpec((group, 2, rows, width), lambda h: (h, 0, 0, 0)),
        out_shape=pltpu.HBM((heads, 2, rows, width), key_rows.dtype),
        compiler_params=pltpu.CompilerParams(vmem_limit_bytes=VMEM),
        name="pack",
    )(
        *(
            pltpu.with_memory_space_constraint(a, pltpu.HBM)
            for a in (key_rows, value_rows, token_rates.T)
        )
    )


def turn_kernel(side_ref, rows_ref, out_ref):
    width = out_ref.shape[3]
    for i in range(out_ref.shape[1]):
        out_ref[0, i] = rows_ref[:, i * width : (i + 1) * width]


def turn(query_rows, side, sides, width):
    rows, columns = query_rows.shape
    strip = columns // sides
    return pl.pallas_call(
        turn_kernel,
        grid_spec=pltpu.PrefetchScalarGridSpec(
            num_scalar_prefetch=1,
            grid=(sides,),
            in_specs=[
                pl.BlockSpec((rows, strip), lambda d, s: (0, lax.rem(s[0] - d + sides, sides)))
            ],
            out_specs=pl.BlockSpec((1, strip // width, rows, width), lambda d, s: (d, 0, 0, 0)),
        ),
        out_shape=jax.ShapeDtypeStruct((sides, strip // width, rows, width), query_rows.dtype),
        compiler_params=pltpu.CompilerParams(vmem_limit_bytes=VMEM),
        cost_estimate=SMALL,
        name="turn",
    )(side[None], pltpu.with_memory_space_constraint(query_rows, pltpu.HBM))


def hold_kernel(start, own_ref, other_ref, after_ref, out_ref, sems):
    core = lax.axis_index("core")
    depth, count = own_ref.shape[0], out_ref.shape[1]
    copies = [
        pltpu.make_async_copy(
            ref.at[:, pl.ds(start, count)], out_ref.at[pl.ds(place * depth, depth)], sems.at[n]
        )
        for n, (ref, place) in enumerate(((own_ref, core), (other_ref, 1 - core)))
    ]
    for copy in copies:
        copy.start()
    for copy in copies:
        copy.wait()


def hold(own, other, start, stop, after):
    depth = own.shape[0]
    own = pltpu.with_memory_space_constraint(own, pltpu.HBM)
    other = pltpu.with_memory_space_constraint(other, pltpu.HBM)
    return pl.pallas_call(
        functools.partial(hold_kernel, start),
        in_specs=[pl.BlockSpec(memory_space=pltpu.HBM)] * 2 + [pl.BlockSpec(memory_space=pl.ANY)],
        out_specs=pl.BlockSpec(memory_space=pltpu.VMEM),
        out_shape=pltpu.VMEM((2 * depth, stop - start), own.dtype),
        scratch_shapes=[pltpu.SemaphoreType.DMA((2,))],
        compiler_params=pltpu.CompilerParams(vmem_limit_bytes=VMEM),
        cost_estimate=SMALL,
        name="hold",
    )(own, other, after)


def gradient_kernel(blocks, tokens_ref, weight_ref, grad_ref):
    w1, w3, w2 = (weight_ref[m].astype(jnp.bfloat16) for m in range(3))
    sources, _, rows, width = tokens_ref.shape
    totals = [None] * 3
    for start in range(0, sources, blocks):
        keys = tokens_ref[start : start + blocks, 0].reshape(blocks * rows, width)
        grad_out = tokens_ref[start : start + blocks, 1].reshape(blocks * rows, width)
        pre = lax.dot_general(w1, keys, NT, preferred_element_type=jnp.float32)
        gate = lax.dot_general(w3, keys, NT, preferred_element_type=jnp.float32)
        grad_hidden = lax.dot_general(w2, grad_out, NT, preferred_element_type=jnp.float32)
        sig = sigmoid(pre)
        silu = pre * sig
        hidden = (silu * gate).astype(jnp.bfloat16)
        grad_pre = (grad_hidden * gate * (sig + silu * (1.0 - sig))).astype(jnp.bfloat16)
        grad_gate = (grad_hidden * silu).astype(jnp.bfloat16)
        parts = (f32_dot(grad_pre, keys), f32_dot(grad_gate, keys), f32_dot(hidden, grad_out))
        totals = [p if t is None else t + p for t, p in zip(totals, parts)]
    for m in range(3):
        grad_ref[m] = totals[m].astype(grad_ref.dtype)


def head_gradient(tokens, weight):
    sources, _, rows, width = tokens.shape
    units = weight.shape[1]
    block = min(256, units)
    return pl.pallas_call(
        functools.partial(gradient_kernel, max(1, min(sources, 512 // rows))),
        grid=(units // block,),
        in_specs=[
            pl.BlockSpec(tokens.shape, lambda f: (0, 0, 0, 0)),
            pl.BlockSpec((3, block, width), lambda f: (0, f, 0)),
        ],
        out_specs=pl.BlockSpec((3, block, width), lambda f: (0, f, 0)),
        out_shape=jax.ShapeDtypeStruct(weight.shape, jnp.bfloat16),
        compiler_params=pltpu.CompilerParams(vmem_limit_bytes=VMEM),
        cost_estimate=SMALL,
        name="head_gradient",
    )(tokens, pltpu.with_memory_space_constraint(weight, pltpu.HBM))


def update_kernel(terms, weight_ref, momentum_ref, *refs):
    out_ref = refs[-1]
    previous = weight_ref[0]
    change = 0.9 * momentum_ref[0]
    for ref in refs[:terms]:
        change = change + ref[0].astype(jnp.float32)
    updated = previous - change

    def scaled(axis):
        old = jnp.sum(jnp.square(previous), axis=axis, keepdims=True)
        new = jnp.sum(jnp.square(updated), axis=axis, keepdims=True)
        out_ref[0] = (updated * (jnp.sqrt(old) / jnp.sqrt(new + 1e-06))).astype(out_ref.dtype)

    @pl.when(pl.program_id(0) < 2)
    def _():
        scaled(1)

    @pl.when(pl.program_id(0) == 2)
    def _():
        scaled(0)


def update(weight, moment, gradients, after):
    _, units, width = weight.shape
    spec = pl.BlockSpec((1, units, width), lambda m: (m, 0, 0))
    return pl.pallas_call(
        functools.partial(update_kernel, len(gradients)),
        grid=(3,),
        in_specs=[spec] * (2 + len(gradients)) + [pl.BlockSpec(memory_space=pl.ANY)] * len(after),
        out_specs=spec,
        out_shape=jax.ShapeDtypeStruct(weight.shape, jnp.bfloat16),
        compiler_params=pltpu.CompilerParams(vmem_limit_bytes=VMEM),
        cost_estimate=SMALL,
        name="update",
    )(weight, moment, *gradients, *after)


def apply_kernel(parts, offsets, normed_ref, query_ref, *refs):
    out_refs = refs[-len(offsets) :]
    head = lax.axis_index("hd")
    _, _, rows, _ = query_ref.shape
    group = max(1, min(len(offsets), 512 // rows))
    for p, part in enumerate(parts):
        for start in range(0, len(offsets), group):
            picked = offsets[start : start + group]
            query = jnp.concatenate(
                [query_ref[jnp.bitwise_xor(head, i), part] for i in picked], axis=0
            )
            pre = lax.dot_general(query, normed_ref[0], NT, preferred_element_type=jnp.float32)
            gate = lax.dot_general(query, normed_ref[1], NT, preferred_element_type=jnp.float32)
            hidden = (pre * sigmoid(pre) * gate).astype(jnp.bfloat16)
            out = f32_dot(hidden, normed_ref[2]).astype(jnp.bfloat16)
            for n in range(len(picked)):
                out_refs[start + n][p] = out[n * rows : (n + 1) * rows]


def apply_head(queries, parts, offsets, normed, after):
    _, _, rows, width = queries.shape
    whole = pl.BlockSpec(memory_space=pltpu.VMEM)
    shape = jax.ShapeDtypeStruct((len(parts), rows, width), jnp.bfloat16)
    return pl.pallas_call(
        functools.partial(apply_kernel, parts, offsets),
        in_specs=[whole, whole] + [pl.BlockSpec(memory_space=pl.ANY)] * len(after),
        out_specs=[whole] * len(offsets),
        out_shape=[shape] * len(offsets),
        compiler_params=pltpu.CompilerParams(vmem_limit_bytes=VMEM),
        cost_estimate=SMALL,
        name="apply_head",
    )(normed, queries, *after)


def project_kernel(places, pieces, *refs):
    terms = len(places)
    mixed_refs, out_ref, depth_ref = refs[:terms], refs[-2], refs[-1]
    head = lax.axis_index("hd")
    for i, (ref, place) in enumerate(zip(mixed_refs, places)):
        depth_ref[jnp.bitwise_xor(head, i)] = ref[place]
    mixed = jnp.concatenate([depth_ref[i] for i in range(terms)], axis=1)
    first = 0
    for weight_ref in refs[terms : terms + pieces]:
        columns = weight_ref.shape[1]
        block = 512 if columns % 512 == 0 else columns
        for start in range(0, columns, block):
            part = f32_dot(mixed, weight_ref[:, start : start + block])
            out_ref[:, first + start : first + start + block] = part.astype(out_ref.dtype)
        first += columns


def project(blocks, weights, dtype, after):
    mixed, places = zip(*blocks)
    _, rows, width = mixed[0].shape
    whole = pl.BlockSpec(memory_space=pltpu.VMEM)
    weights = [pltpu.with_memory_space_constraint(w, pltpu.VMEM) for w in weights]
    return pl.pallas_call(
        functools.partial(project_kernel, places, len(weights)),
        in_specs=[whole] * (len(mixed) + len(weights))
        + [pl.BlockSpec(memory_space=pl.ANY)] * len(after),
        out_specs=whole,
        out_shape=jax.ShapeDtypeStruct((rows, sum(w.shape[1] for w in weights)), dtype),
        scratch_shapes=[pltpu.VMEM((len(mixed), rows, width), mixed[0].dtype)],
        compiler_params=pltpu.CompilerParams(vmem_limit_bytes=VMEM),
        cost_estimate=SMALL,
        name="project",
    )(*mixed, *weights, *after)


def finish_kernel(places, pieces, *refs):
    terms = len(places)
    mixed_refs, weight_refs = refs[:terms], refs[terms : terms + pieces]
    received_refs = refs[terms + pieces : -3]
    out_ref, rest_ref, depth_ref = refs[-3:]
    head = lax.axis_index("hd")
    for i, (ref, place) in enumerate(zip(mixed_refs, places)):
        depth_ref[jnp.bitwise_xor(head, i)] = ref[place]
    mixed = jnp.concatenate([depth_ref[i] for i in range(terms)], axis=1)
    for weight_ref in weight_refs:
        columns = weight_ref.shape[1]
        block = 512 if columns % 512 == 0 else columns
        for start in range(0, columns, block):
            part = f32_dot(mixed, weight_ref[:, start : start + block])
            if weight_ref is weight_refs[0]:
                for ref in received_refs:
                    part = part + ref[:, start : start + block].astype(jnp.float32)
                out_ref[:, start : start + block] = part.astype(out_ref.dtype)
            else:
                rest_ref[:, start : start + block] = part


def finish(blocks, weights, received):
    mixed, places = zip(*blocks)
    _, rows, width = mixed[0].shape
    whole = pl.BlockSpec(memory_space=pltpu.VMEM)
    first, last = (w.shape[1] for w in weights)
    weights = [pltpu.with_memory_space_constraint(w, pltpu.VMEM) for w in weights]
    return pl.pallas_call(
        functools.partial(finish_kernel, places, len(weights)),
        in_specs=[whole] * (len(mixed) + len(weights) + len(received)),
        out_specs=[whole] * 2,
        out_shape=[
            jax.ShapeDtypeStruct((rows, first + last), jnp.bfloat16),
            jax.ShapeDtypeStruct((rows, last), jnp.float32),
        ],
        scratch_shapes=[pltpu.VMEM((len(mixed), rows, width), mixed[0].dtype)],
        compiler_params=pltpu.CompilerParams(vmem_limit_bytes=VMEM),
        cost_estimate=SMALL,
        name="finish",
    )(*mixed, *weights, *received)


def close_kernel(whole_ref, rest_ref, *refs):
    total = rest_ref[...]
    for ref in refs[:-1]:
        total = total + ref[...].astype(jnp.float32)
    refs[-1][...] = total.astype(refs[-1].dtype)


def close(result, rest, received):
    rows, columns = rest.shape
    place = result.shape[1] // columns - 1
    block = pl.BlockSpec((rows, columns), lambda n: (0, 0))
    return pl.pallas_call(
        close_kernel,
        grid=(1,),
        in_specs=[pl.BlockSpec(memory_space=pl.ANY)] + [block] * (1 + len(received)),
        out_specs=pl.BlockSpec((rows, columns), lambda n: (0, place)),
        out_shape=jax.ShapeDtypeStruct(result.shape, result.dtype),
        input_output_aliases={0: 0},
        compiler_params=pltpu.CompilerParams(vmem_limit_bytes=VMEM),
        cost_estimate=SMALL,
        name="close",
    )(result, rest, *received)


def shards(query_rows, key_rows, value_rows, token_rates, fast_weights, momentum, out_weight):
    sides, heads_here = lax.axis_size("x"), lax.axis_size("hd")
    side, core, head = lax.axis_index("x"), lax.axis_index("core"), lax.axis_index("hd")
    copies = lax.axis_size("rep")
    per_device, _, units, width = fast_weights.shape
    rows = key_rows.shape[0]
    rate_scale = float(rows * sides * 2 * heads_here * copies) ** (-0.5)
    swap = [(0, 1), (1, 0)]

    payload = pack(key_rows, value_rows, token_rates, width, rate_scale)
    tokens = lax.all_to_all(payload, ("x", "hd"), 0, 0, tiled=True)

    owned = head // per_device == core
    weight = lax.dynamic_index_in_dim(fast_weights, head % per_device, 0, keepdims=False)
    moment = lax.dynamic_index_in_dim(momentum, head % per_device, 0, keepdims=False)
    weight = jnp.where(owned, weight, lax.ppermute(weight, "core", swap))
    moment = jnp.where(owned, moment, lax.ppermute(moment, "core", swap))
    out_weight_other = lax.ppermute(out_weight, "core", swap)

    turned = turn(query_rows, side, sides, width)
    query_parts = [turned[0]] + [
        lax.ppermute(turned[d], "x", [(i, (i - d) % sides) for i in range(sides)])
        for d in range(1, sides)
    ]
    ready = jnp.stack(query_parts, axis=1)
    ready, weight, moment, tokens = lax.optimization_barrier((ready, weight, moment, tokens))
    queries = lax.all_to_all(ready, "hd", 0, 0, tiled=True)

    gradient = head_gradient(tokens, weight)
    gradients = [gradient, lax.ppermute(gradient, "core", swap)]
    if copies > 1:
        summed = gradients[0].astype(jnp.float32) + gradients[1].astype(jnp.float32)
        gradients = [lax.psum(summed.astype(jnp.bfloat16), "rep")]
    normed = update(weight, moment, gradients, [])
    half = heads_here // 2
    near, far = tuple([*range(1, half), 0]), tuple(range(half, heads_here))
    partner = [[(c, c ^ i) for c in range(heads_here)] for i in range(heads_here)]

    columns = out_weight.shape[1]
    split = columns * 3 // 4
    steps = (*range(1, sides), 0)

    def spread(parts, offsets, after):
        applied = apply_head(queries, parts, offsets, normed, after)
        moved = [
            lax.ppermute(block, "hd", partner[i]) if i else block
            for i, block in zip(offsets, applied)
        ]
        return moved, applied[0]

    crossing, done = {}, None
    crossing[steps[0]], done = spread(steps[:1], far, [])
    local, done = spread(steps, near, [done])
    held = [hold(out_weight, out_weight_other, 0, split, done)]
    crossing[steps[1]], done = spread(steps[1:2], far, held)
    received = [[], []]
    for place, step in enumerate(steps):
        if step not in crossing:
            crossing[step], done = spread((step,), far, [done])
        blocks = [None] * heads_here
        for i, block in zip(near, local):
            blocks[i] = (block, place)
        for i, block in zip(far, crossing[step]):
            blocks[i] = (block, 0)
        if step:
            over = [(i, (i + step) % sides) for i in range(sides)]
            done = project(blocks, held[:1], jnp.bfloat16, [done])
            received[0].append(lax.ppermute(done, "x", over))
            if len(held) == 1:
                held.append(hold(out_weight, out_weight_other, split, columns, done))
            done = project(blocks, held[1:], jnp.bfloat16, [])
            received[1].append(lax.ppermute(done, "x", over))
        else:
            result, rest = finish(blocks, held, received[0])
    return close(result, rest, received[1])


def solution(mesh):
    head_axis, ctx_axis = mesh.shape["head"], mesh.shape["ctx"]

    def run(query_rows, key_rows, value_rows, token_rates, fast_weights, momentum, out_weight):
        heads_here = fast_weights.shape[0] // (head_axis // 2)
        fine = Mesh(
            mesh.devices.reshape(head_axis // 2, 2, heads_here, ctx_axis // heads_here),
            ("x", "core", "hd", "rep"),
        )
        token_spec = P(("x", "core", "hd", "rep"), None)
        weight_spec = P(("x", "core"), None, None, None)
        return jax.shard_map(
            shards,
            mesh=fine,
            in_specs=(token_spec,) * 4 + (weight_spec, weight_spec, P(("x", "core"), None)),
            out_specs=token_spec,
            check_vma=False,
        )(query_rows, key_rows, value_rows, token_rates, fast_weights, momentum, out_weight)

    return run
```
